512 devices in a mesh: dp: 8 (over x, core), tensor: 8 (over z), vocab: 8 (over y).
Axes of the slice: x: 4, y: 8, z: 8, core: 2. Of those that a mesh axis runs over, the one named last changes fastest.
Arguments:
- hidden_in: bfloat16 [1024, 4608], P('dp')
- norm_pre: float32 [4608], replicated, may hold values from 0.1 to 1.9
- w_gate: bfloat16 [4608, 18432], P('dp', ('tensor', 'vocab')), may hold values from -0.09375 to 0.09375
- w_up: bfloat16 [4608, 18432], P('dp', ('tensor', 'vocab')), may hold values from -0.09375 to 0.09375
- w_down: bfloat16 [18432, 4608], P(('tensor', 'vocab'), 'dp'), may hold values from -0.125 to 0.125
- norm_post: float32 [4608], replicated, may hold values from 0.1 to 1.9
- norm_final: float32 [4608], replicated, may hold values from 0.1 to 1.9
- unembed: bfloat16 [4608, 131072], P(None, ('dp', 'tensor', 'vocab')), may hold values from -0.375 to 0.375
- token_ids: int32 [1024], P('dp'), may hold values from 0 to 131071
- lengths: int32 [16], P('dp'), may hold values from 1 to 63, as said below
Outputs:
- token_logprob: float32 [1024], P('dp')
The draws below stay inside these ranges and needn't reach their ends.
Inputs may be any that keep to these rules, and one draw needn't show every extreme that they name: The rollouts are numbered by index of dp, 2 to each; the lengths of the rollouts of one index of dp sum to at most 64, and to exactly 64 on at least one index of dp, whose rollouts have lengths 64 - 1 and 1.
All inputs are finite; a program needn't handle non-finite values.
Results may differ from the reference program's by a relative error of at most 0.0035.
Values may be sent and summed in bfloat16 or wider, within the bound.
A program may use at most 64 MiB of HBM per device.

```python
import math
import jax
import jax.numpy as jnp
import numpy as np
from jax import lax

D = 4608
FF = 18432
VOCAB = 131072
TOK_DEV = 128
SEQS = 2
SEG = 64
LIVE_CAP = 64
TOKENS = 1024
ROLLOUTS = 16
N_DP = 8


def draw_hidden_in(key, part):
    key_rows, key_cols, key_base = jax.random.split(key, 3)
    ramp = jnp.exp(math.log(3.0) * jnp.arange(D, dtype=jnp.float32) / D)[None, :]
    row_scale = jnp.exp(jax.random.uniform(key_rows, (TOKENS, 1), jnp.float32, 0.0, math.log(10.0)))
    col_scale = jnp.exp(jax.random.uniform(key_cols, (1, D), jnp.float32, 0.0, math.log(4.0))) * ramp
    base = jax.random.normal(key_base, (TOKENS, D), jnp.float32)
    return (0.25 * base * row_scale * col_scale).astype(jnp.bfloat16)


def draw_lengths(key, part):
    key_total, key_full, key_weight = jax.random.split(key, 3)
    groups = ROLLOUTS // SEQS
    totals = jax.random.randint(key_total, (groups,), SEQS, LIVE_CAP + 1)
    fullest = jax.random.randint(key_full, (), 0, groups)
    full_row = jnp.arange(groups) == fullest
    totals = jnp.where(full_row, LIVE_CAP, totals)
    weights = jax.random.randint(key_weight, (groups, SEQS), 1, 1000)
    lopsided = jnp.where(jnp.arange(SEQS)[None, :] == 0, 1000, 0).astype(jnp.int32)
    weights = jnp.where(full_row[:, None], lopsided, weights)
    extra = totals - SEQS
    shares = extra[:, None] * weights // jnp.sum(weights, axis=1, keepdims=True)
    shares = shares.at[:, 0].add(extra - jnp.sum(shares, axis=1))
    return (1 + shares).reshape(ROLLOUTS).astype(jnp.int32)


def touch_ends(result, key, least, top_value):
    dims = result.shape
    index_at = [jax.random.randint(jax.random.fold_in(key, axis), (), 0, dims[axis]) for axis in range(len(dims))]
    result = result.at[tuple(index_at)].set(least)
    longest = dims.index(max(dims))
    index_at[longest] = (index_at[longest] + 1) % dims[longest]
    return result.at[tuple(index_at)].set(top_value)


def with_spikes(array, stream_key, source, target, blocks, factor):
    def block_of(position):
        return (jnp.arange(array.shape[position]) // (array.shape[position] // blocks)).reshape((-1,) + (1,) * (array.ndim - 1 - position))

    first = jax.random.permutation(stream_key, blocks)[block_of(target)]
    far = (block_of(target) + blocks // 2) % blocks
    return jnp.where((block_of(source) == first) | (block_of(source) == far), factor * array, array)


def block_scale(stream_key, shape, cuts, smallest, top_value):
    def one(position, parts):
        steps = jax.random.uniform(jax.random.fold_in(jax.random.fold_in(stream_key, 6), position), (parts,), jnp.float32, smallest / len(cuts), top_value / len(cuts))
        return jnp.repeat(jnp.exp(steps), shape[position] // parts).reshape((-1,) + (1,) * (len(shape) - position - 1))

    factor_of = one(*cuts[0])
    for cut in cuts[1:]:
        factor_of = factor_of * one(*cut)
    return factor_of


def ranked_wide(stream_key, shape, count, slope):
    portions = [min(1 << octave, count + 1 - (1 << octave)) * (1 << 20) // math.isqrt((1 << octave) ** slope) + 1 for octave in range((count + 1).bit_length()) if 1 << octave <= count]
    width = 1 + sum(portions) // (1 << 30)
    grid = np.cumsum(np.array([max(1, weight // width) for weight in portions]))
    pick = jax.random.randint(jax.random.fold_in(stream_key, 1), shape, 0, int(grid[len(portions) - 1]))
    start = jnp.left_shift(1, jnp.searchsorted(jnp.asarray(grid, jnp.int32), pick, side="right").astype(jnp.int32))
    grade = start - 1 + jax.random.randint(jax.random.fold_in(stream_key, 4), shape, 0, 1 << 30) % jnp.minimum(start, count + 1 - start)
    return jax.random.permutation(jax.random.fold_in(stream_key, 2), count)[grade].astype(jnp.int32)


def scatter_about(key, extent, spread, most, pieces=(), kind=jnp.bfloat16):
    gain = block_scale(key, extent, pieces, -0.22, 0.18) if pieces else 1.0
    array = jax.random.normal(key, extent, jnp.float32) * spread * gain
    return jnp.minimum(jnp.maximum(array, -most), most).astype(kind)


def noise_with(own_key, extent, spread, bound, pieces, heavy, kind=jnp.bfloat16):
    values = spread * jax.random.normal(own_key, extent, jnp.float32)
    if pieces:
        values = values * block_scale(own_key, extent, pieces, -0.22, 0.18)
    return jnp.clip(with_spikes(values, jax.random.fold_in(own_key, 3), *heavy), -bound, bound).astype(kind)


def setup_inputs(seed: int = 0) -> dict:
    splits = jax.random.split(jax.random.key(seed), 11)
    return {
        "hidden_in": draw_hidden_in(jax.random.fold_in(splits[10], 71), 0),
        "norm_pre": jnp.clip(1.0 + 0.18 * jax.random.normal(splits[1], (D,), jnp.float32), 0.1, 1.9),
        "w_gate": scatter_about(splits[2], (D, FF), D ** -0.5, 0.09375, ((0, 8), (1, 64))),
        "w_up": scatter_about(splits[3], (D, FF), D ** -0.5, 0.09375, ((0, 8), (1, 64))),
        "w_down": noise_with(splits[4], (FF, D), FF ** -0.5, 0.125, ((0, 64), (1, 8)), (0, 1, 64, 4.0)),
        "norm_post": jnp.clip(1.0 + 0.18 * jax.random.normal(splits[5], (D,), jnp.float32), 0.1, 1.9),
        "norm_final": jnp.clip(1.0 + 0.18 * jax.random.normal(splits[6], (D,), jnp.float32), 0.1, 1.9),
        "unembed": scatter_about(splits[7], (D, VOCAB), (D // 16) ** -0.5, 0.375, ((1, 512),)),
        "token_ids": touch_ends(ranked_wide(splits[8], (TOKENS,), VOCAB, 2), jax.random.fold_in(splits[8], 3), 0, VOCAB - 1).astype(jnp.int32),
        "lengths": draw_lengths(jax.random.fold_in(splits[10], 71), 0),
    }


EPS = 1e-06
CAP = 30.0

def rms_scale(values):
    return lax.rsqrt(lax.optimization_barrier(jnp.mean(values * values, axis=-1, keepdims=True)) + EPS)

def reference(hidden_in, norm_pre, w_gate, w_up, w_down, norm_post, norm_final, unembed, token_ids, lengths):
    stream_in = hidden_in.astype(jnp.float32)
    normed = (stream_in * rms_scale(stream_in) * norm_pre).astype(jnp.bfloat16)
    feature_block = D // N_DP
    gate = jnp.zeros((TOKENS, FF), jnp.float32)
    upward = jnp.zeros((TOKENS, FF), jnp.float32)
    for number in range(N_DP):
        lower = number * feature_block
        upper = lower + feature_block
        taken = normed[:, lower:upper]
        gate_part = jnp.dot(taken, w_gate[lower:upper], preferred_element_type=jnp.float32).astype(jnp.bfloat16)
        up_part = jnp.dot(taken, w_up[lower:upper], preferred_element_type=jnp.float32).astype(jnp.bfloat16)
        gate_part, up_part = lax.optimization_barrier((gate_part, up_part))
        gate = gate + gate_part.astype(jnp.float32)
        upward = upward + up_part.astype(jnp.float32)
    hidden = (jax.nn.silu(gate) * upward).astype(jnp.bfloat16)
    branch = jnp.dot(hidden, w_down, preferred_element_type=jnp.float32)
    stream = stream_in + branch * rms_scale(branch) * norm_post
    final = (stream * rms_scale(stream) * norm_final).astype(jnp.bfloat16)
    columns = min(VOCAB, 8192)

    def vocab_step(carry, number):
        totals, targets = carry
        start = (number * columns).astype(jnp.int32)
        table = lax.dynamic_slice_in_dim(unembed, start, columns, 1)
        capped = CAP * jnp.tanh(jnp.dot(final, table, preferred_element_type=jnp.float32) / CAP)
        totals = totals + lax.optimization_barrier(jnp.sum(jnp.exp(capped - CAP), axis=1))
        matches = jnp.arange(columns, dtype=jnp.int32)[None, :] + start == token_ids[:, None]
        targets = targets + lax.optimization_barrier(jnp.sum(jnp.where(matches, capped, jnp.float32(0.0)), axis=1))
        return ((totals, targets), None)
    initial = (jnp.zeros((TOKENS,), jnp.float32), jnp.zeros((TOKENS,), jnp.float32))
    (totals, targets), _ = lax.scan(vocab_step, initial, jnp.arange(VOCAB // columns, dtype=jnp.int32))
    slots = jnp.arange(TOKENS, dtype=jnp.int32)
    rollout = (slots // TOK_DEV * SEQS + slots % TOK_DEV // SEG).astype(jnp.int32)
    bounds = lengths[rollout]
    scored = slots % SEG < bounds
    return jnp.where(scored, targets - CAP - jnp.log(totals), jnp.float32(0.0))
```

```python
import functools

import jax
import jax.numpy as jnp
from jax import lax
from jax.experimental import pallas as pl
from jax.experimental.pallas import tpu as pltpu
from jax.sharding import PartitionSpec as P

EPS = 1e-06
CAP = 30.0
LIVE = 64
MESH = pl.DeviceIdType.MESH
BF = jnp.bfloat16
F32 = jnp.float32
LAST = (((1,), (1,)), ((), ()))


def far_first(n):
    order = []
    for step in range(n // 2, 0, -1):
        order.append(step)
        if n - step != step:
            order.append(n - step)
    return order


def near_first(n):
    return far_first(n)[::-1]


def kernel(
    cfg,
    hid_hbm, pre_hbm, post_hbm, fin_hbm, wg_hbm, wu_hbm, wd_hbm, un_hbm, tok_hbm, len_hbm,
    out_ref,
    hid, gains, tok_ref, len_ref, hs, hx, wgu, wd2, wd, un,
    own, ps, pr, hb, bs, r1, s1, r2, st, sr, fa, fb, tk, fs, fx, fyb, fy, fzb, fz,
    l_sem, c_ssem, c_rsem, a_ssem, a_rsem, t_ssem, t_rsem, p_ssem, p_rsem, h_ssem, h_rsem,
    b1_ssem, b1_rsem, b2_ssem, b2_rsem, n_ssem, n_rsem, ga_ssem, ga_rsem, gb_ssem, gb_rsem,
    rr_ssem, rr_rsem, rl_ssem, rl_rsem, gx_ssem, gx_rsem, fx_ssem, fx_rsem, fy_ssem, fy_rsem, fz_ssem, fz_rsem,
):
    NX, NY, NZ, D, U, VS = cfg
    DC = D // NX
    DH = DC // 2
    NG = NY
    E = NG // NX
    GR = NX * LIVE // (2 * NG)
    DA = fa.shape[-1]
    TOK = hid.shape[0]
    dp = lax.axis_index("dp")
    z = lax.axis_index("tensor")
    y = lax.axis_index("vocab")
    x = dp // 2
    c = dp % 2

    def xpeer(k):
        return {"dp": lax.rem(dp + 2 * k, 2 * NX)}

    def ypeer(k):
        return {"vocab": lax.rem(y + k, NY)}

    def zpeer(k):
        return {"tensor": lax.rem(z + k, NZ)}

    core = {"dp": dp + 1 - 2 * c}
    here = (y, z)
    first = (ypeer, zpeer)
    second = (zpeer, ypeer)

    def rcopy(src, dst, ss, rs, dev):
        return pltpu.make_async_remote_copy(
            src_ref=src, dst_ref=dst, send_sem=ss, recv_sem=rs, device_id=dev, device_id_type=MESH
        )

    sent = []

    def go(copy):
        copy.start()
        sent.append(copy)
        return copy

    far_x = far_first(NX)
    near_x = near_first(NX)
    far_y = far_first(NY)

    tok_in = pltpu.make_async_copy(tok_hbm, tok_ref, l_sem.at[NX + 7])
    len_in = pltpu.make_async_copy(len_hbm, len_ref, l_sem.at[NX + 8])
    len_in.start()
    tok_in.start()
    hid_in = []
    for n, k in enumerate(far_x + [0]):
        cols = pl.ds(pl.multiple_of(lax.rem(x + k, NX) * DC, 128), DC)
        cp = pltpu.make_async_copy(hid_hbm.at[:, cols], hid.at[:, cols], l_sem.at[n])
        cp.start()
        hid_in.append((k, cols, cp))
    w_in = [
        pltpu.make_async_copy(wg_hbm, wgu.at[c, 0:U], l_sem.at[NX]),
        pltpu.make_async_copy(wu_hbm, wgu.at[c, U:2 * U], l_sem.at[NX + 1]),
        pltpu.make_async_copy(wd_hbm, wd2.at[c], l_sem.at[NX + 2]),
        pltpu.make_async_copy(un_hbm, un.at[c], l_sem.at[NX + 3]),
    ]
    for cp in w_in:
        cp.start()
    gain_in = []
    for n, src in enumerate((pre_hbm, post_hbm, fin_hbm)):
        cp = pltpu.make_async_copy(src, gains.at[n], l_sem.at[NX + 4 + n])
        cp.start()
        gain_in.append(cp)

    def gain(n):
        gain_in[n].wait()
        lines = DC // 128
        return jnp.concatenate([gains[n, pl.ds(x * lines + i, 1)] for i in range(lines)], axis=1)

    barrier = pltpu.get_barrier_semaphore()
    partners = [core] + [xpeer(k) for k in range(1, NX)] + [ypeer(k) for k in range(1, NY)] + [zpeer(k) for k in range(1, NZ)]
    for dev in partners:
        pl.semaphore_signal(barrier, inc=1, device_id=dev, device_id_type=MESH)

    len_in.wait()
    l0 = len_ref[0]
    l1 = len_ref[1]
    prow = lax.broadcasted_iota(jnp.int32, (LIVE, TOK), 0)
    scol = lax.broadcasted_iota(jnp.int32, (LIVE, TOK), 1)
    origin = jnp.where(prow < l0, prow, jnp.where(prow < l0 + l1, prow - l0 + LIVE, -1))
    pick = scol == origin
    keep = jnp.where(pick, 1.0, 0.0).astype(BF)
    eye_low = scol == prow
    eye_high = scol == prow + LIVE

    pl.semaphore_wait(barrier, len(partners))

    w_out = [
        rcopy(wg_hbm, wgu.at[c, 0:U], c_ssem.at[0], c_rsem.at[0], core),
        rcopy(wu_hbm, wgu.at[c, U:2 * U], c_ssem.at[1], c_rsem.at[1], core),
        rcopy(wd_hbm, wd2.at[c], c_ssem.at[2], c_rsem.at[2], core),
        rcopy(un_hbm, un.at[c], c_ssem.at[3], c_rsem.at[3], core),
    ]
    go(w_out[0])
    go(w_out[1])

    square = jnp.zeros((LIVE, 1), F32)
    a_cp = {}
    for k, cols, cp in hid_in:
        cp.wait()
        part = jnp.dot(keep, hid[:, cols], preferred_element_type=F32)
        cut = part.astype(BF)
        if k == 0:
            for q in range(2 * E):
                hx[x, q] = cut[q * GR:(q + 1) * GR]
        else:
            for q in range(2 * E):
                hs[k - 1, q] = cut[q * GR:(q + 1) * GR]
            a_cp[k] = go(rcopy(hs.at[k - 1], hx.at[x], a_ssem.at[k - 1], a_rsem.at[k - 1], xpeer(k)))
        square = square + jnp.sum(part * part, axis=1, keepdims=True)
    go(w_out[2])
    go(w_out[3])
    scale = lax.rsqrt(square / D + EPS)

    tok_in.wait()
    toks = jnp.sum(jnp.where(pick, tok_ref[...].astype(F32), 0.0), axis=1, keepdims=True)
    tok_row = jnp.sum(jnp.where(eye_low, toks, 0.0), axis=0, keepdims=True)
    tk[x] = jnp.broadcast_to(tok_row, (8, TOK))
    t_cp = {}
    for k in range(1, NX):
        t_cp[k] = go(rcopy(tk.at[x], tk.at[x], t_ssem.at[k - 1], t_rsem.at[k - 1], xpeer(k)))

    gain_pre = gain(0)
    for n in range(2):
        w_in[n].wait()
        w_out[n].wait_recv()
    p_cp = {}
    for k in [0] + near_x:
        j = lax.rem(x - k + NX, NX)
        if k:
            a_cp[k].wait_recv()
        rows = hx[j].reshape(LIVE, DC).astype(F32)
        rows = (rows * gain_pre).astype(BF)
        part = lax.dot_general(rows[:, 0:DH], wgu[0], LAST, preferred_element_type=F32)
        part = part + lax.dot_general(rows[:, DH:DC], wgu[1], LAST, preferred_element_type=F32)
        if k == 0:
            own[...] = part
        else:
            ps[k - 1] = part.astype(BF)
            p_cp[k] = go(rcopy(ps.at[k - 1], pr.at[k - 1], p_ssem.at[k - 1], p_rsem.at[k - 1], xpeer(NX - k)))

    w_in[2].wait()
    w_out[2].wait_recv()
    wd[:, 0:DH] = wd2[0]
    wd[:, DH:DC] = wd2[1]

    both = own[...]
    for k in near_x:
        p_cp[k].wait_recv()
        both = both + pr[k - 1].astype(F32)
    both = jnp.where(scale > 0.0, both * scale, 0.0)
    gate = both[:, 0:U]
    up = both[:, U:2 * U]
    hb[x] = (gate / (1.0 + jnp.exp(-gate)) * up).astype(BF)
    h_cp = {}
    for k in far_x:
        h_cp[k] = go(rcopy(hb.at[x], hb.at[x], h_ssem.at[k - 1], h_rsem.at[k - 1], xpeer(k)))

    for k in [0] + near_x:
        j = lax.rem(x - k + NX, NX)
        if k:
            h_cp[k].wait_recv()
        part = jnp.dot(hb[j], wd[...], preferred_element_type=F32).astype(BF)
        for half in range(2):
            for e in range(E):
                q = half * E + e
                bs[half, j * E + e] = part[q * GR:(q + 1) * GR]
    b1_cp = {}
    for k in far_y:
        for half in range(2):
            g = lax.rem(here[half] + k, NG)
            b1_cp[half, k] = go(rcopy(
                bs.at[half, g], r1.at[half, k - 1], b1_ssem.at[half, k - 1], b1_rsem.at[half, k - 1], first[half](k)
            ))
    b2_cp = {}
    for half in range(2):
        total = bs[half, here[half]].astype(F32)
        for k in near_first(NY):
            b1_cp[half, k].wait_recv()
            total = total + r1[half, k - 1].astype(F32)
        s1[half] = total.astype(BF)
        for k in far_y:
            b2_cp[half, k] = go(rcopy(
                s1.at[half], r2.at[half, k - 1], b2_ssem.at[half, k - 1], b2_rsem.at[half, k - 1], second[half](k)
            ))

    gain_post = gain(1)
    gain_final = gain(2)
    lane = lax.broadcasted_iota(jnp.int32, (GR, 128), 1)
    halves = []
    for half in range(2):
        branch = s1[half].astype(F32)
        for k in near_first(NY):
            b2_cp[half, k].wait_recv()
            branch = branch + r2[half, k - 1].astype(F32)
        rows = hx[here[half] // E, half * E + here[half] % E].astype(F32)
        scaled = branch * gain_post
        sums = jnp.where(lane == 0, jnp.sum(branch * branch, axis=1, keepdims=True), 0.0)
        sums = jnp.where(lane == 1, jnp.sum(rows * scaled, axis=1, keepdims=True), sums)
        sums = jnp.where(lane == 2, jnp.sum(scaled * scaled, axis=1, keepdims=True), sums)
        sums = jnp.where(lane == 3, jnp.sum(rows * rows, axis=1, keepdims=True), sums)
        st[half] = sums
        halves.append((rows, scaled))
    n_cp = {}
    for k in far_x:
        n_cp[k] = go(rcopy(st, sr.at[k - 1], n_ssem.at[k - 1], n_rsem.at[k - 1], xpeer(k)))
    all_sums = [st[half] for half in range(2)]
    for k in near_x:
        n_cp[k].wait_recv()
        all_sums = [all_sums[half] + sr[k - 1, half] for half in range(2)]
    ga_cp = {}
    gb_cp = {}
    for half in range(2):
        sums = all_sums[half]
        rows, scaled = halves[half]
        factor = lax.rsqrt(sums[:, 0:1] / D + EPS)
        spread = sums[:, 3:4] + factor * (2.0 * sums[:, 1:2] + factor * sums[:, 2:3])
        inverse = lax.rsqrt(jnp.maximum(spread, 0.0) / D + EPS)
        final = ((rows + scaled * factor) * inverse * gain_final).astype(BF)
        g = here[half]
        fa[half, g, x] = final[:, 0:DA]
        fb[half, x, g] = final[:, DA:DC]
        for k in far_x:
            ga_cp[half, k] = go(rcopy(
                fa.at[half, g, x], fa.at[half, g, x], ga_ssem.at[half, k - 1], ga_rsem.at[half, k - 1], xpeer(k)
            ))
        for k in far_y:
            gb_cp[half, k] = go(rcopy(
                fb.at[half, x, g], fb.at[half, x, g], gb_ssem.at[half, k - 1], gb_rsem.at[half, k - 1], first[half](k)
            ))

    rings = {}

    def ring(half, s):
        g = here[half]
        up_g = lax.rem(g - s + NG, NG)
        down_g = lax.rem(g + s, NG)
        if s < NG // 2 - 1:
            a = (fa.at[half, up_g], fa.at[half, down_g])
        else:
            a = (fa.at[half, up_g, 0:NX // 2], fa.at[half, down_g, NX // 2:NX])
        rings[half, s] = (
            go(rcopy(a[0], a[0], rr_ssem.at[half, s], rr_rsem.at[half, s], first[half](1))),
            go(rcopy(a[1], a[1], rl_ssem.at[half, s], rl_rsem.at[half, s], first[half](NG - 1))),
        )

    def ring_wait(half, s):
        for cp in rings[half, s]:
            cp.wait_recv()

    for half in range(2):
        for k in near_x:
            ga_cp[half, k].wait_recv()
        ring(half, 0)
    gx_cp = {}
    for half in range(2):
        for k in near_first(NY):
            gb_cp[half, k].wait_recv()
        for k in far_x:
            gx_cp[half, k] = go(rcopy(
                fb.at[half, x], fb.at[half, x], gx_ssem.at[half, k - 1], gx_rsem.at[half, k - 1], xpeer(k)
            ))
    for s in range(1, NG // 2):
        for half in range(2):
            ring_wait(half, s - 1)
            ring(half, s)

    w_in[3].wait()
    w_out[3].wait_recv()
    for k in range(1, NX):
        t_cp[k].wait_recv()
    tok_cols = [jnp.sum(jnp.where(eye_low, tk[j, 0:1], 0.0), axis=1, keepdims=True) for j in range(NX)]
    HR = LIVE // 2
    entry = lax.broadcasted_iota(jnp.int32, (NG * GR, VS), 1).astype(F32)
    totals = []
    targets = []
    for half in range(2):
        ring_wait(half, NG // 2 - 1)
        for k in near_x:
            gx_cp[half, k].wait_recv()
        tok_half = jnp.concatenate([t[half * HR:(half + 1) * HR] for t in tok_cols], axis=0)
        total = jnp.zeros((NG * GR, 1), F32)
        target = jnp.zeros((NG * GR, 1), F32)
        for which in range(2):
            logits = jnp.zeros((NG * GR, VS), F32)
            for j in range(NX):
                logits = logits + jnp.dot(
                    fa[half, :, j].reshape(NG * GR, DA), un[which, j * DC:j * DC + DA], preferred_element_type=F32
                )
                logits = logits + jnp.dot(
                    fb[half, j].reshape(NG * GR, DC - DA), un[which, j * DC + DA:(j + 1) * DC], preferred_element_type=F32
                )
            capped = CAP * jnp.tanh(logits / CAP)
            offset = (((x * 2 + which) * NZ + z) * NY + y) * VS
            total = total + jnp.sum(jnp.exp(capped - CAP), axis=1, keepdims=True)
            target = target + jnp.sum(
                jnp.where(entry == tok_half - offset.astype(F32), capped, 0.0), axis=1, keepdims=True
            )
        totals.append(total)
        targets.append(target)

    for j in range(NX):
        t = jnp.concatenate([v[j * HR:(j + 1) * HR] for v in totals], axis=0)
        g = jnp.concatenate([v[j * HR:(j + 1) * HR] for v in targets], axis=0)
        row = jnp.sum(jnp.where(eye_low, t, 0.0) + jnp.where(eye_high, g, 0.0), axis=0, keepdims=True)
        fs[j] = jnp.broadcast_to(row, (8, TOK))
    fx_cp = {}
    for k in far_x:
        fx_cp[k] = go(rcopy(fs.at[lax.rem(x + k, NX)], fx.at[k - 1], fx_ssem.at[k - 1], fx_rsem.at[k - 1], xpeer(k)))
    acc = fs[x]
    for k in near_x:
        fx_cp[k].wait_recv()
        acc = acc + fx[k - 1]
    fyb[...] = acc
    fy_cp = {}
    for k in far_y:
        fy_cp[k] = go(rcopy(fyb, fy.at[k - 1], fy_ssem.at[k - 1], fy_rsem.at[k - 1], ypeer(k)))
    for k in near_first(NY):
        fy_cp[k].wait_recv()
        acc = acc + fy[k - 1]
    fzb[...] = acc
    fz_cp = {}
    for k in far_y:
        fz_cp[k] = go(rcopy(fzb, fz.at[k - 1], fz_ssem.at[k - 1], fz_rsem.at[k - 1], zpeer(k)))
    for k in near_first(NY):
        fz_cp[k].wait_recv()
        acc = acc + fz[k - 1]
    row = acc[0:1]
    t = jnp.sum(jnp.where(eye_low, row, 0.0), axis=1, keepdims=True)
    g = jnp.sum(jnp.where(eye_high, row, 0.0), axis=1, keepdims=True)
    logprob = g - CAP - jnp.log(t)
    out_ref[...] = jnp.sum(jnp.where(pick, logprob, 0.0), axis=0, keepdims=True)
    for cp in sent:
        cp.wait_send()


def solution(mesh):
    NX = mesh.shape["dp"] // 2
    NY = mesh.shape["vocab"]
    NZ = mesh.shape["tensor"]

    def on_device(
        hidden_in, norm_pre, w_gate, w_up, w_down, norm_post, norm_final, unembed, token_ids, lengths
    ):
        TOK, D = hidden_in.shape
        U = w_gate.shape[1]
        VS = unembed.shape[1]
        DC = D // NX
        DH = DC // 2
        DA = DC // 3 * 2
        NG = NY
        GR = NX * LIVE // (2 * NG)
        E = NG // NX
        cfg = (NX, NY, NZ, D, U, VS)
        any_spec = pl.BlockSpec(memory_space=pl.ANY)
        vmem = pl.BlockSpec(memory_space=pltpu.VMEM)
        dma = lambda *s: pltpu.SemaphoreType.DMA(s)
        xs = NX - 1
        ys = NY - 1
        pairs = lambda *s: [dma(*s), dma(*s)]
        lines = lambda v: v.reshape(D // 128, 128)
        out = pl.pallas_call(
            functools.partial(kernel, cfg),
            out_shape=jax.ShapeDtypeStruct((1, TOK), F32),
            in_specs=[any_spec] * 10,
            out_specs=vmem,
            scratch_shapes=[
                pltpu.VMEM((TOK, D), BF),
                pltpu.VMEM((3, D // 128, 128), F32),
                pltpu.VMEM((1, TOK), jnp.int32),
                pltpu.SMEM((2,), jnp.int32),
                pltpu.VMEM((xs, 2 * E, GR, DC), BF),
                pltpu.VMEM((NX, 2 * E, GR, DC), BF),
                pltpu.VMEM((2, 2 * U, DH), BF),
                pltpu.VMEM((2, U, DH), BF),
                pltpu.VMEM((U, DC), BF),
                pltpu.VMEM((2, D, VS), BF),
                pltpu.VMEM((LIVE, 2 * U), F32),
                pltpu.VMEM((xs, LIVE, 2 * U), BF),
                pltpu.VMEM((xs, LIVE, 2 * U), BF),
                pltpu.VMEM((NX, LIVE, U), BF),
                pltpu.VMEM((2, NG, GR, DC), BF),
                pltpu.VMEM((2, ys, GR, DC), BF),
                pltpu.VMEM((2, GR, DC), BF),
                pltpu.VMEM((2, ys, GR, DC), BF),
                pltpu.VMEM((2, GR, 128), F32),
                pltpu.VMEM((xs, 2, GR, 128), F32),
                pltpu.VMEM((2, NG, NX, GR, DA), BF),
                pltpu.VMEM((2, NX, NG, GR, DC - DA), BF),
                pltpu.VMEM((NX, 8, TOK), F32),
                pltpu.VMEM((NX, 8, TOK), F32),
                pltpu.VMEM((xs, 8, TOK), F32),
                pltpu.VMEM((8, TOK), F32),
                pltpu.VMEM((ys, 8, TOK), F32),
                pltpu.VMEM((8, TOK), F32),
                pltpu.VMEM((ys, 8, TOK), F32),
                dma(NX + 9),
            ]
            + pairs(4) + pairs(xs) + pairs(xs) + pairs(xs) + pairs(xs)
            + pairs(2, ys) + pairs(2, ys) + pairs(xs) + pairs(2, xs) + pairs(2, ys)
            + pairs(2, NG // 2) + pairs(2, NG // 2) + pairs(2, xs) + pairs(xs) + pairs(ys) + pairs(ys),
            compiler_params=pltpu.CompilerParams(
                collective_id=0, has_side_effects=True, vmem_limit_bytes=60 * 1024 * 1024
            ),
            name="rollout_logprob",
        )(
            hidden_in, lines(norm_pre), lines(norm_post), lines(norm_final), w_gate.T, w_up.T, w_down, unembed,
            token_ids.reshape(1, TOK), lengths,
        )
        return out.reshape(TOK)

    in_specs = (
        P("dp", None),
        P(),
        P("dp", ("tensor", "vocab")),
        P("dp", ("tensor", "vocab")),
        P(("tensor", "vocab"), "dp"),
        P(),
        P(),
        P(None, ("dp", "tensor", "vocab")),
        P("dp"),
        P("dp"),
    )
    return jax.shard_map(
        on_device, mesh=mesh, in_specs=in_specs, out_specs=P("dp"), check_vma=False
    )
```

```python
import functools

import jax
import jax.numpy as jnp
from jax import lax
from jax.experimental import pallas as pl
from jax.experimental.pallas import tpu as pltpu
from jax.sharding import PartitionSpec as P

EPS = 1e-06
CAP = 30.0
HOPS = (0, 1, 2, 3)
PIECES = 4
LIVE = 64
MESH = pl.DeviceIdType.MESH
BF = jnp.bfloat16
F32 = jnp.float32
LAST = (((1,), (1,)), ((), ()))


def far_first(n):
    order = []
    for step in range(n // 2, 0, -1):
        order.append(step)
        if n - step != step:
            order.append(n - step)
    return order


def near_first(n):
    return far_first(n)[::-1]


def kernel(
    cfg,
    hid_hbm, pre_hbm, post_hbm, fin_hbm, wg_hbm, wu_hbm, wd_hbm, un_hbm, tok_hbm, len_hbm,
    out_ref,
    hid, gains, tok_ref, len_ref, hs, hx, wgu, wd2, wd, un,
    own, ps, pr, hb, bs, r1, s1, r2, hrow, bx, flow, fa, lg, tk, fs, fx, fyb, fy, fzb, fz,
    l_sem, c_ssem, c_rsem, a_ssem, a_rsem, t_ssem, t_rsem, p_ssem, p_rsem, h_ssem, h_rsem,
    b1_ssem, b1_rsem, b2_ssem, b2_rsem, n_ssem, n_rsem, q_ssem, q_rsem,
    rr_ssem, rr_rsem, fx_ssem, fx_rsem, fy_ssem, fy_rsem, fz_ssem, fz_rsem,
):
    NX, NY, NZ, D, U, VS = cfg
    DC = D // NX
    DH = DC // 2
    NG = NY
    E = NG // NX
    GR = NX * LIVE // (2 * NG)
    TOK = hid.shape[0]
    dp = lax.axis_index("dp")
    z = lax.axis_index("tensor")
    y = lax.axis_index("vocab")
    x = dp // 2
    c = dp % 2

    def xpeer(k):
        return {"dp": lax.rem(dp + 2 * k, 2 * NX)}

    def ypeer(k):
        return {"vocab": lax.rem(y + k, NY)}

    def zpeer(k):
        return {"tensor": lax.rem(z + k, NZ)}

    core = {"dp": dp + 1 - 2 * c}
    here = (y, z)
    first = (ypeer, zpeer)
    second = (zpeer, ypeer)

    def rcopy(src, dst, ss, rs, dev):
        return pltpu.make_async_remote_copy(
            src_ref=src, dst_ref=dst, send_sem=ss, recv_sem=rs, device_id=dev, device_id_type=MESH
        )

    sent = []

    def drain(keep=0):
        while len(sent) > keep:
            sent.pop(0).wait_send()

    def go(copy):
        copy.start()
        sent.append(copy)
        return copy

    far_x = far_first(NX)
    near_x = near_first(NX)
    far_y = far_first(NY)

    barrier = pltpu.get_barrier_semaphore()
    partners = [core] + [xpeer(k) for k in range(1, NX)] + [ypeer(k) for k in range(1, NY)] + [zpeer(k) for k in range(1, NZ)]
    for dev in partners:
        pl.semaphore_signal(barrier, inc=1, device_id=dev, device_id_type=MESH)

    tok_in = pltpu.make_async_copy(tok_hbm, tok_ref, l_sem.at[NX + 7])
    len_in = pltpu.make_async_copy(len_hbm, len_ref, l_sem.at[NX + 8])
    len_in.start()
    hid_in = []
    for n, k in enumerate(far_x + [0]):
        cols = pl.ds(pl.multiple_of(lax.rem(x + k, NX) * DC, 128), DC)
        cp = pltpu.make_async_copy(hid_hbm.at[:, cols], hid.at[:, cols], l_sem.at[n])
        cp.start()
        hid_in.append((k, cols, cp))
    tok_in.start()
    w_in = [
        pltpu.make_async_copy(wg_hbm, wgu.at[c, 0:U], l_sem.at[NX]),
        pltpu.make_async_copy(wu_hbm, wgu.at[c, U:2 * U], l_sem.at[NX + 1]),
        pltpu.make_async_copy(wd_hbm, wd2.at[c], l_sem.at[NX + 2]),
        pltpu.make_async_copy(un_hbm, un.at[c], l_sem.at[NX + 3]),
    ]
    for cp in w_in:
        cp.start()
    gain_in = []
    for n, src in enumerate((pre_hbm, post_hbm, fin_hbm)):
        cp = pltpu.make_async_copy(src, gains.at[n], l_sem.at[NX + 4 + n])
        cp.start()
        gain_in.append(cp)

    def gain(n, j):
        lines = DC // 128
        return jnp.concatenate([gains[n, pl.ds(j * lines + i, 1)] for i in range(lines)], axis=1)

    len_in.wait()
    l0 = len_ref[0]
    l1 = len_ref[1]
    prow = lax.broadcasted_iota(jnp.int32, (LIVE, TOK), 0)
    scol = lax.broadcasted_iota(jnp.int32, (LIVE, TOK), 1)
    origin = jnp.where(prow < l0, prow, jnp.where(prow < l0 + l1, prow - l0 + LIVE, -1))
    pick = scol == origin
    keep = jnp.where(pick, 1.0, 0.0).astype(BF)
    eye_low = scol == prow
    eye_high = scol == prow + LIVE

    pl.semaphore_wait(barrier, len(partners))

    w_out = [
        rcopy(wg_hbm, wgu.at[c, 0:U], c_ssem.at[0], c_rsem.at[0], core),
        rcopy(wu_hbm, wgu.at[c, U:2 * U], c_ssem.at[1], c_rsem.at[1], core),
        rcopy(wd_hbm, wd2.at[c], c_ssem.at[2], c_rsem.at[2], core),
        rcopy(un_hbm, un.at[c], c_ssem.at[3], c_rsem.at[3], core),
    ]
    go(w_out[0])
    go(w_out[1])

    square = jnp.zeros((LIVE, 1), F32)
    a_cp = {}
    for k, cols, cp in hid_in:
        cp.wait()
        part = jnp.dot(keep, hid[:, cols], preferred_element_type=F32)
        cut = part.astype(BF)
        if k == 0:
            for q in range(2 * E):
                hx[x, q] = cut[q * GR:(q + 1) * GR]
        else:
            for q in range(2 * E):
                hs[k - 1, q] = cut[q * GR:(q + 1) * GR]
            a_cp[k] = go(rcopy(hs.at[k - 1], hx.at[x], a_ssem.at[k - 1], a_rsem.at[k - 1], xpeer(k)))
        square = square + jnp.sum(part * part, axis=1, keepdims=True)
    go(w_out[2])
    go(w_out[3])
    scale = lax.rsqrt(square / D + EPS)

    tok_in.wait()
    toks = jnp.sum(jnp.where(pick, tok_ref[...].astype(F32), 0.0), axis=1, keepdims=True)
    tok_row = jnp.sum(jnp.where(eye_low, toks, 0.0), axis=0, keepdims=True)
    tk[x] = jnp.broadcast_to(tok_row, (8, TOK))
    t_cp = {}
    for k in range(1, NX):
        t_cp[k] = go(rcopy(tk.at[x], tk.at[x], t_ssem.at[k - 1], t_rsem.at[k - 1], xpeer(k)))

    gain_in[0].wait()
    gain_pre = gain(0, x)
    for n in range(2):
        w_in[n].wait()
        w_out[n].wait_recv()
    p_cp = {}
    for k in [0] + near_x:
        j = lax.rem(x - k + NX, NX)
        if k:
            a_cp[k].wait_recv()
        rows = hx[j].reshape(LIVE, DC).astype(F32)
        rows = (rows * gain_pre).astype(BF)
        part = lax.dot_general(rows[:, 0:DH], wgu[0], LAST, preferred_element_type=F32)
        part = part + lax.dot_general(rows[:, DH:DC], wgu[1], LAST, preferred_element_type=F32)
        if k == 0:
            own[...] = part
        else:
            ps[k - 1] = part.astype(BF)
            p_cp[k] = go(rcopy(ps.at[k - 1], pr.at[k - 1], p_ssem.at[k - 1], p_rsem.at[k - 1], xpeer(NX - k)))

    w_in[2].wait()
    w_out[2].wait_recv()
    wd[:, 0:DH] = wd2[0]
    wd[:, DH:DC] = wd2[1]

    both = own[...]
    for k in near_x:
        p_cp[k].wait_recv()
        both = both + pr[k - 1].astype(F32)
    both = jnp.where(scale > 0.0, both * scale, 0.0)
    gate = both[:, 0:U]
    up = both[:, U:2 * U]
    hb[x] = (gate / (1.0 + jnp.exp(-gate)) * up).astype(BF)
    h_cp = {}
    for k in far_x:
        h_cp[k] = go(rcopy(hb.at[x], hb.at[x], h_ssem.at[k - 1], h_rsem.at[k - 1], xpeer(k)))

    b1_cp = {}
    for half in range(2):
        for k in far_y:
            g = lax.rem(here[half] + k, NG)
            b1_cp[half, k] = rcopy(
                bs.at[half, g], r1.at[half, k - 1], b1_ssem.at[half, k - 1], b1_rsem.at[half, k - 1], first[half](k)
            )
    for k in [0] + near_x:
        j = lax.rem(x - k + NX, NX)
        if k:
            h_cp[k].wait_recv()
        part = jnp.dot(hb[j], wd[...], preferred_element_type=F32).astype(BF)
        for half in range(2):
            for e in range(E):
                q = half * E + e
                bs[half, e * NX + j] = part[q * GR:(q + 1) * GR]
        for half in range(2):
            for e in range(E):
                away = lax.rem(e * NX + j - here[half] + NG, NG)

                @pl.when(away > 0)
                def _(half=half, g=e * NX + j, away=away):
                    rcopy(
                        bs.at[half, g], r1.at[half, away - 1], b1_ssem.at[half, away - 1], b1_rsem.at[half, away - 1],
                        {"vocab": g} if half == 0 else {"tensor": g},
                    ).start()
    sent.extend(b1_cp[half, k] for half in range(2) for k in far_y)
    for half in range(2):
        q = half * E + here[half] // NX

        @pl.when(x == lax.rem(here[half], NX))
        def _(half=half, q=q):
            hrow[half, x] = hx[x, q]
            for k in range(1, NX):
                hrow[half, lax.rem(x + k, NX)] = hs[k - 1, q]
            for k in far_x:
                rcopy(hrow.at[half], hrow.at[half], q_ssem.at[half, k - 1], q_rsem.at[half], xpeer(k)).start()

    drain(keep=14)
    b2_cp = {}
    for half in range(2):
        total = bs[half, here[half]].astype(F32)
        for k in near_first(NY):
            b1_cp[half, k].wait_recv()
            total = total + r1[half, k - 1].astype(F32)
        s1[half] = total.astype(BF)
        for k in far_y:
            b2_cp[half, k] = go(rcopy(
                s1.at[half], r2.at[half, k - 1], b2_ssem.at[half, k - 1], b2_rsem.at[half, k - 1], second[half](k)
            ))

    drain(keep=14)
    bx_cp = {}
    for half in range(2):
        branch = s1[half].astype(F32)
        for k in near_first(NY):
            b2_cp[half, k].wait_recv()
            branch = branch + r2[half, k - 1].astype(F32)
        bx[half, x] = branch.astype(BF)
        for k in far_x:
            bx_cp[half, k] = go(rcopy(
                bx.at[half, x], bx.at[half, x], n_ssem.at[half, k - 1], n_rsem.at[half, k - 1], xpeer(k)
            ))
    gain_in[1].wait()
    gain_in[2].wait()
    for half in range(2):
        whole = rcopy(hrow.at[half], hrow.at[half], q_ssem.at[half, 0], q_rsem.at[half], xpeer(1))

        @pl.when(x != lax.rem(here[half], NX))
        def _(whole=whole):
            whole.wait_recv()

        @pl.when(x == lax.rem(here[half], NX))
        def _(half=half):
            for k in far_x:
                rcopy(hrow.at[half], hrow.at[half], q_ssem.at[half, k - 1], q_rsem.at[half], xpeer(k)).wait_send()

    for half in range(2):
        for k in near_x:
            bx_cp[half, k].wait_recv()
        branches = [bx[half, j].astype(F32) for j in range(NX)]
        square = sum(jnp.sum(b * b, axis=1, keepdims=True) for b in branches)
        factor = lax.rsqrt(square / D + EPS)
        square = jnp.zeros((GR, 1), F32)
        for j in range(NX):
            stream = hrow[half, j].astype(F32) + branches[j] * factor * gain(1, j)
            flow[half, j] = stream
            square = square + jnp.sum(stream * stream, axis=1, keepdims=True)
        inverse = lax.rsqrt(square / D + EPS)
        for j in range(NX):
            fa[half, here[half], j] = (flow[half, j] * inverse * gain(2, j)).astype(BF)

    last = NG // 2 - 1
    source = HOPS
    pieces = PIECES
    width = NX // pieces
    rings = {}
    got = set()

    def arrived(*key):
        if key not in got:
            got.add(key)
            rings[key].wait_recv()

    def runs(s, i, way):
        return s < last or (i < pieces // 2) == (way == 0)

    def ring(s, i):
        near = source[s]
        for half in range(2):
            for way in range(2):
                if near:
                    arrived(half, near - 1, i, way)
                if runs(s, i, way):
                    block = fa.at[half, lax.rem(here[half] + (near if way else NG - near), NG), pl.ds(i * width, width)]
                    hops = s + 1 - near
                    rings[half, s, i, way] = go(rcopy(
                        block, block, rr_ssem.at[half, s, i, way], rr_rsem.at[half, s, i, way],
                        first[half](NG - hops if way else hops)
                    ))

    def multiply(shifts):
        picks = []
        for half in range(2):
            for shift in shifts:
                for i in range(pieces):
                    for way in range(2):
                        if shift and runs(shift - 1, i, way):
                            arrived(half, shift - 1, i, way)
                for sign in sorted({shift % NG, -shift % NG}):
                    picks.append((half, lax.rem(here[half] + sign, NG)))
        lhs = [jnp.concatenate([fa[h, g, j] for h, g in picks], axis=0) for j in range(NX)]
        for which in range(2):
            total = jnp.dot(lhs[0], un[which, 0:DC], preferred_element_type=F32)
            for j in range(1, NX):
                total = total + jnp.dot(lhs[j], un[which, j * DC:(j + 1) * DC], preferred_element_type=F32)
            for n, (h, g) in enumerate(picks):
                lg[which, h, g] = total[n * GR:(n + 1) * GR]

    for s in range(NG // 2):
        for i in range(pieces):
            ring(s, i)
        if s == 0:
            w_in[3].wait()
            w_out[3].wait_recv()
    for k in range(1, NX):
        t_cp[k].wait_recv()
    tok_cols = [jnp.sum(jnp.where(eye_low, tk[j, 0:1], 0.0), axis=1, keepdims=True) for j in range(NX)]
    multiply([0, 1] if last > 0 else [0])
    drain(keep=40)
    for s in range(2, NG // 2):
        multiply([s])
    multiply([NG // 2])
    HR = LIVE // 2
    entry = lax.broadcasted_iota(jnp.int32, (NG * GR, VS), 1).astype(F32)
    totals = []
    targets = []
    for half in range(2):
        tok_half = jnp.concatenate(
            [t[half * HR + e * GR:half * HR + (e + 1) * GR] for e in range(E) for t in tok_cols], axis=0
        )
        total = jnp.zeros((NG * GR, 1), F32)
        target = jnp.zeros((NG * GR, 1), F32)
        for which in range(2):
            logits = lg[which, half].reshape(NG * GR, VS)
            capped = CAP * jnp.tanh(logits / CAP)
            offset = (((x * 2 + which) * NZ + z) * NY + y) * VS
            total = total + jnp.sum(jnp.exp(capped - CAP), axis=1, keepdims=True)
            target = target + jnp.sum(
                jnp.where(entry == tok_half - offset.astype(F32), capped, 0.0), axis=1, keepdims=True
            )
        totals.append(total)
        targets.append(target)

    for j in range(NX):
        spans = [(half, (e * NX + j) * GR) for half in range(2) for e in range(E)]
        t = jnp.concatenate([totals[half][at:at + GR] for half, at in spans], axis=0)
        g = jnp.concatenate([targets[half][at:at + GR] for half, at in spans], axis=0)
        row = jnp.sum(jnp.where(eye_low, t, 0.0) + jnp.where(eye_high, g, 0.0), axis=0, keepdims=True)
        fs[j] = jnp.broadcast_to(row, (8, TOK))
    fx_cp = {}
    for k in far_x:
        fx_cp[k] = go(rcopy(fs.at[lax.rem(x + k, NX)], fx.at[k - 1], fx_ssem.at[k - 1], fx_rsem.at[k - 1], xpeer(k)))
    acc = fs[x]
    for k in near_x:
        fx_cp[k].wait_recv()
        acc = acc + fx[k - 1]
    drain(keep=3)
    fyb[...] = acc
    fy_cp = {}
    for k in far_y:
        fy_cp[k] = go(rcopy(fyb, fy.at[k - 1], fy_ssem.at[k - 1], fy_rsem.at[k - 1], ypeer(k)))
    for k in near_first(NY):
        fy_cp[k].wait_recv()
        acc = acc + fy[k - 1]
    fzb[...] = acc
    fz_cp = {}
    for k in far_y:
        fz_cp[k] = go(rcopy(fzb, fz.at[k - 1], fz_ssem.at[k - 1], fz_rsem.at[k - 1], zpeer(k)))
    for k in near_first(NY):
        fz_cp[k].wait_recv()
        acc = acc + fz[k - 1]
    row = acc[0:1]
    t = jnp.sum(jnp.where(eye_low, row, 0.0), axis=1, keepdims=True)
    g = jnp.sum(jnp.where(eye_high, row, 0.0), axis=1, keepdims=True)
    logprob = g - CAP - jnp.log(t)
    out_ref[...] = jnp.sum(jnp.where(pick, logprob, 0.0), axis=0, keepdims=True)
    drain()


def solution(mesh):
    NX = mesh.shape["dp"] // 2
    NY = mesh.shape["vocab"]
    NZ = mesh.shape["tensor"]

    def on_device(
        hidden_in, norm_pre, w_gate, w_up, w_down, norm_post, norm_final, unembed, token_ids, lengths
    ):
        TOK, D = hidden_in.shape
        U = w_gate.shape[1]
        VS = unembed.shape[1]
        DC = D // NX
        DH = DC // 2
        NG = NY
        GR = NX * LIVE // (2 * NG)
        E = NG // NX
        cfg = (NX, NY, NZ, D, U, VS)
        any_spec = pl.BlockSpec(memory_space=pl.ANY)
        vmem = pl.BlockSpec(memory_space=pltpu.VMEM)
        dma = lambda *s: pltpu.SemaphoreType.DMA(s)
        xs = NX - 1
        ys = NY - 1
        pairs = lambda *s: [dma(*s), dma(*s)]
        lines = lambda v: v.reshape(D // 128, 128)
        out = pl.pallas_call(
            functools.partial(kernel, cfg),
            out_shape=jax.ShapeDtypeStruct((1, TOK), F32),
            in_specs=[any_spec] * 10,
            out_specs=vmem,
            scratch_shapes=[
                pltpu.VMEM((TOK, D), BF),
                pltpu.VMEM((3, D // 128, 128), F32),
                pltpu.VMEM((1, TOK), jnp.int32),
                pltpu.SMEM((2,), jnp.int32),
                pltpu.VMEM((xs, 2 * E, GR, DC), BF),
                pltpu.VMEM((NX, 2 * E, GR, DC), BF),
                pltpu.VMEM((2, 2 * U, DH), BF),
                pltpu.VMEM((2, U, DH), BF),
                pltpu.VMEM((U, DC), BF),
                pltpu.VMEM((2, D, VS), BF),
                pltpu.VMEM((LIVE, 2 * U), F32),
                pltpu.VMEM((xs, LIVE, 2 * U), BF),
                pltpu.VMEM((xs, LIVE, 2 * U), BF),
                pltpu.VMEM((NX, LIVE, U), BF),
                pltpu.VMEM((2, NG, GR, DC), BF),
                pltpu.VMEM((2, ys, GR, DC), BF),
                pltpu.VMEM((2, GR, DC), BF),
                pltpu.VMEM((2, ys, GR, DC), BF),
                pltpu.VMEM((2, NX, GR, DC), BF),
                pltpu.VMEM((2, NX, GR, DC), BF),
                pltpu.VMEM((2, NX, GR, DC), F32),
                pltpu.VMEM((2, NG, NX, GR, DC), BF),
                pltpu.VMEM((2, 2, NG, GR, VS), F32),
                pltpu.VMEM((NX, 8, TOK), F32),
                pltpu.VMEM((NX, 8, TOK), F32),
                pltpu.VMEM((xs, 8, TOK), F32),
                pltpu.VMEM((8, TOK), F32),
                pltpu.VMEM((ys, 8, TOK), F32),
                pltpu.VMEM((8, TOK), F32),
                pltpu.VMEM((ys, 8, TOK), F32),
                dma(NX + 9),
            ]
            + pairs(4) + pairs(xs) + pairs(xs) + pairs(xs) + pairs(xs)
            + pairs(2, ys) + pairs(2, ys) + pairs(2, xs) + [dma(2, xs), dma(2)]
            + pairs(2, NG // 2, NX, 2) + pairs(xs) + pairs(ys) + pairs(ys),
            compiler_params=pltpu.CompilerParams(
                collective_id=0, has_side_effects=True, vmem_limit_bytes=60 * 1024 * 1024
            ),
            name="rollout_logprob",
        )(
            hidden_in, lines(norm_pre), lines(norm_post), lines(norm_final), w_gate.T, w_up.T, w_down, unembed,
            token_ids.reshape(1, TOK), lengths,
        )
        return out.reshape(TOK)

    in_specs = (
        P("dp", None),
        P(),
        P("dp", ("tensor", "vocab")),
        P("dp", ("tensor", "vocab")),
        P(("tensor", "vocab"), "dp"),
        P(),
        P(),
        P(None, ("dp", "tensor", "vocab")),
        P("dp"),
        P("dp"),
    )
    return jax.shard_map(
        on_device, mesh=mesh, in_specs=in_specs, out_specs=P("dp"), check_vma=False
    )
```

```python
import functools

import jax
import jax.numpy as jnp
from jax import lax
from jax.experimental import pallas as pl
from jax.experimental.pallas import tpu as pltpu
from jax.sharding import PartitionSpec as P

EPS = 1e-06
CAP = 30.0
HOPS = (0, 1, 2, 3)
PIECES = 4
LIVE = 64
MESH = pl.DeviceIdType.MESH
BF = jnp.bfloat16
F32 = jnp.float32
LAST = (((1,), (1,)), ((), ()))


def far_first(n):
    order = []
    for step in range(n // 2, 0, -1):
        order.append(step)
        if n - step != step:
            order.append(n - step)
    return order


def near_first(n):
    return far_first(n)[::-1]


def kernel(
    cfg,
    hid_hbm, pre_hbm, post_hbm, fin_hbm, wg_hbm, wu_hbm, wd_hbm, un_hbm, tok_hbm, len_hbm,
    out_ref,
    hid, gains, tok_ref, len_ref, hs, hx, wgu, wd2, wd, un,
    own, ps, pr, hb, bs, r1, s1, r2, hrow, bx, flow, fa, lg, tk, fs, fx, fyb, fy, fzb, fz,
    l_sem, c_ssem, c_rsem, a_ssem, a_rsem, t_ssem, t_rsem, p_ssem, p_rsem, h_ssem, h_rsem,
    b1_ssem, b1_rsem, b2_ssem, b2_rsem, n_ssem, n_rsem, q_ssem, q_rsem,
    rr_ssem, rr_rsem, fx_ssem, fx_rsem, fy_ssem, fy_rsem, fz_ssem, fz_rsem,
):
    NX, NY, NZ, D, U, VS = cfg
    DC = D // NX
    DH = DC // 2
    NG = NY
    E = NG // NX
    GR = NX * LIVE // (2 * NG)
    TOK = hid.shape[0]
    dp = lax.axis_index("dp")
    z = lax.axis_index("tensor")
    y = lax.axis_index("vocab")
    x = dp // 2
    c = dp % 2

    def xpeer(k):
        return {"dp": lax.rem(dp + 2 * k, 2 * NX)}

    def ypeer(k):
        return {"vocab": lax.rem(y + k, NY)}

    def zpeer(k):
        return {"tensor": lax.rem(z + k, NZ)}

    core = {"dp": dp + 1 - 2 * c}
    here = (y, z)
    first = (ypeer, zpeer)
    second = (zpeer, ypeer)

    def rcopy(src, dst, ss, rs, dev):
        return pltpu.make_async_remote_copy(
            src_ref=src, dst_ref=dst, send_sem=ss, recv_sem=rs, device_id=dev, device_id_type=MESH
        )

    sent = []

    def drain(keep=0):
        while len(sent) > keep:
            sent.pop(0).wait_send()

    def go(copy):
        copy.start()
        sent.append(copy)
        return copy

    far_x = far_first(NX)
    near_x = near_first(NX)
    far_y = far_first(NY)

    barrier = pltpu.get_barrier_semaphore()
    partners = [core] + [xpeer(k) for k in range(1, NX)] + [ypeer(k) for k in range(1, NY)] + [zpeer(k) for k in range(1, NZ)]
    for dev in partners:
        pl.semaphore_signal(barrier, inc=1, device_id=dev, device_id_type=MESH)

    tok_in = pltpu.make_async_copy(tok_hbm, tok_ref, l_sem.at[NX + 7])
    len_in = pltpu.make_async_copy(len_hbm, len_ref, l_sem.at[NX + 8])
    len_in.start()
    hid_in = []
    for n, k in enumerate(far_x + [0]):
        cols = pl.ds(pl.multiple_of(lax.rem(x + k, NX) * DC, 128), DC)
        cp = pltpu.make_async_copy(hid_hbm.at[:, cols], hid.at[:, cols], l_sem.at[n])
        cp.start()
        hid_in.append((k, cols, cp))
    tok_in.start()
    w_in = [
        pltpu.make_async_copy(wg_hbm, wgu.at[c, 0:U], l_sem.at[NX]),
        pltpu.make_async_copy(wu_hbm, wgu.at[c, U:2 * U], l_sem.at[NX + 1]),
        pltpu.make_async_copy(wd_hbm, wd2.at[c], l_sem.at[NX + 2]),
        pltpu.make_async_copy(un_hbm, un.at[c], l_sem.at[NX + 3]),
    ]
    for cp in w_in:
        cp.start()
    gain_in = []
    for n, src in enumerate((pre_hbm, post_hbm, fin_hbm)):
        cp = pltpu.make_async_copy(src, gains.at[n], l_sem.at[NX + 4 + n])
        cp.start()
        gain_in.append(cp)

    def gain(n, j):
        lines = DC // 128
        return jnp.concatenate([gains[n, pl.ds(j * lines + i, 1)] for i in range(lines)], axis=1)

    len_in.wait()
    l0 = len_ref[0]
    l1 = len_ref[1]
    prow = lax.broadcasted_iota(jnp.int32, (LIVE, TOK), 0)
    scol = lax.broadcasted_iota(jnp.int32, (LIVE, TOK), 1)
    origin = jnp.where(prow < l0, prow, jnp.where(prow < l0 + l1, prow - l0 + LIVE, -1))
    pick = scol == origin
    keep = jnp.where(pick, 1.0, 0.0).astype(BF)
    eye_low = scol == prow
    eye_high = scol == prow + LIVE

    pl.semaphore_wait(barrier, len(partners))

    w_out = [
        rcopy(wg_hbm, wgu.at[c, 0:U], c_ssem.at[0], c_rsem.at[0], core),
        rcopy(wu_hbm, wgu.at[c, U:2 * U], c_ssem.at[1], c_rsem.at[1], core),
        rcopy(wd_hbm, wd2.at[c], c_ssem.at[2], c_rsem.at[2], core),
        rcopy(un_hbm, un.at[c], c_ssem.at[3], c_rsem.at[3], core),
    ]
    go(w_out[0])
    go(w_out[1])

    square = jnp.zeros((LIVE, 1), F32)
    a_cp = {}
    for k, cols, cp in hid_in:
        cp.wait()
        part = jnp.dot(keep, hid[:, cols], preferred_element_type=F32)
        cut = part.astype(BF)
        if k == 0:
            for q in range(2 * E):
                hx[x, q] = cut[q * GR:(q + 1) * GR]
        else:
            for q in range(2 * E):
                hs[k - 1, q] = cut[q * GR:(q + 1) * GR]
            a_cp[k] = go(rcopy(hs.at[k - 1], hx.at[x], a_ssem.at[k - 1], a_rsem.at[k - 1], xpeer(k)))
        square = square + jnp.sum(part * part, axis=1, keepdims=True)
    go(w_out[2])
    go(w_out[3])
    scale = lax.rsqrt(square / D + EPS)

    tok_in.wait()
    toks = jnp.sum(jnp.where(pick, tok_ref[...].astype(F32), 0.0), axis=1, keepdims=True)
    tok_row = jnp.sum(jnp.where(eye_low, toks, 0.0), axis=0, keepdims=True)
    tk[x] = jnp.broadcast_to(tok_row, (8, TOK))
    t_cp = {}
    for k in range(1, NX):
        t_cp[k] = go(rcopy(tk.at[x], tk.at[x], t_ssem.at[k - 1], t_rsem.at[k - 1], xpeer(k)))

    gain_in[0].wait()
    gain_pre = gain(0, x)
    for n in range(2):
        w_in[n].wait()
        w_out[n].wait_recv()
    p_cp = {}
    batches = [[0], [1, NX - 1], [2]] if NX == 4 else [[k] for k in [0] + near_x]
    for batch in batches:
        rows = []
        for k in batch:
            if k:
                a_cp[k].wait_recv()
            rows.append(hx[lax.rem(x - k + NX, NX)].reshape(LIVE, DC).astype(F32))
        rows = (jnp.concatenate(rows, axis=0) * gain_pre).astype(BF)
        part = lax.dot_general(rows[:, 0:DH], wgu[0], LAST, preferred_element_type=F32)
        part = part + lax.dot_general(rows[:, DH:DC], wgu[1], LAST, preferred_element_type=F32)
        for n, k in enumerate(batch):
            if k == 0:
                own[...] = part
            else:
                ps[k - 1] = part[n * LIVE:(n + 1) * LIVE].astype(BF)
                p_cp[k] = go(rcopy(ps.at[k - 1], pr.at[k - 1], p_ssem.at[k - 1], p_rsem.at[k - 1], xpeer(NX - k)))

    w_in[2].wait()
    w_out[2].wait_recv()
    wd[:, 0:DH] = wd2[0]
    wd[:, DH:DC] = wd2[1]

    both = own[...]
    for k in near_x:
        p_cp[k].wait_recv()
        both = both + pr[k - 1].astype(F32)
    both = jnp.where(scale > 0.0, both * scale, 0.0)
    gate = both[:, 0:U]
    up = both[:, U:2 * U]
    hb[x] = (gate / (1.0 + jnp.exp(-gate)) * up).astype(BF)
    h_cp = {}
    for k in far_x:
        h_cp[k] = go(rcopy(hb.at[x], hb.at[x], h_ssem.at[k - 1], h_rsem.at[k - 1], xpeer(k)))

    b1_cp = {}
    for half in range(2):
        for k in far_y:
            g = lax.rem(here[half] + k, NG)
            b1_cp[half, k] = rcopy(
                bs.at[half, g], r1.at[half, k - 1], b1_ssem.at[half, k - 1], b1_rsem.at[half, k - 1], first[half](k)
            )
    for k in [0] + near_x:
        j = lax.rem(x - k + NX, NX)
        if k:
            h_cp[k].wait_recv()
        part = jnp.dot(hb[j], wd[...], preferred_element_type=F32).astype(BF)
        for half in range(2):
            for e in range(E):
                q = half * E + e
                bs[half, e * NX + j] = part[q * GR:(q + 1) * GR]
        for half in range(2):
            for e in range(E):
                away = lax.rem(e * NX + j - here[half] + NG, NG)

                @pl.when(away > 0)
                def _(half=half, g=e * NX + j, away=away):
                    rcopy(
                        bs.at[half, g], r1.at[half, away - 1], b1_ssem.at[half, away - 1], b1_rsem.at[half, away - 1],
                        {"vocab": g} if half == 0 else {"tensor": g},
                    ).start()
    sent.extend(b1_cp[half, k] for half in range(2) for k in far_y)
    for half in range(2):
        q = half * E + here[half] // NX

        @pl.when(x == lax.rem(here[half], NX))
        def _(half=half, q=q):
            hrow[half, x] = hx[x, q]
            for k in range(1, NX):
                hrow[half, lax.rem(x + k, NX)] = hs[k - 1, q]
            for k in far_x:
                rcopy(hrow.at[half], hrow.at[half], q_ssem.at[half, k - 1], q_rsem.at[half], xpeer(k)).start()

    drain(keep=14)
    b2_cp = {}
    for half in range(2):
        total = bs[half, here[half]].astype(F32)
        for k in near_first(NY):
            b1_cp[half, k].wait_recv()
            total = total + r1[half, k - 1].astype(F32)
        s1[half] = total.astype(BF)
        for k in far_y:
            b2_cp[half, k] = go(rcopy(
                s1.at[half], r2.at[half, k - 1], b2_ssem.at[half, k - 1], b2_rsem.at[half, k - 1], second[half](k)
            ))

    drain(keep=14)
    bx_cp = {}
    for half in range(2):
        branch = s1[half].astype(F32)
        for k in near_first(NY):
            b2_cp[half, k].wait_recv()
            branch = branch + r2[half, k - 1].astype(F32)
        bx[half, x] = branch.astype(BF)
        for k in far_x:
            bx_cp[half, k] = go(rcopy(
                bx.at[half, x], bx.at[half, x], n_ssem.at[half, k - 1], n_rsem.at[half, k - 1], xpeer(k)
            ))
    last = NG // 2 - 1
    source = HOPS
    pieces = PIECES
    width = NX // pieces
    rings = {}
    got = set()

    def arrived(*key):
        if key not in got:
            got.add(key)
            rings[key].wait_recv()

    def runs(s, i, way):
        return s < last or (i < pieces // 2) == (way == 0)

    def ring(s, i, halves=(0, 1)):
        near = source[s]
        for half in halves:
            for way in range(2):
                if near:
                    arrived(half, near - 1, i, way)
                if runs(s, i, way):
                    block = fa.at[half, lax.rem(here[half] + (near if way else NG - near), NG), pl.ds(i * width, width)]
                    hops = s + 1 - near
                    rings[half, s, i, way] = go(rcopy(
                        block, block, rr_ssem.at[half, s, i, way], rr_rsem.at[half, s, i, way],
                        first[half](NG - hops if way else hops)
                    ))

    def multiply(shifts):
        picks = []
        for half in range(2):
            for shift in shifts:
                for i in range(pieces):
                    for way in range(2):
                        if shift and runs(shift - 1, i, way):
                            arrived(half, shift - 1, i, way)
                for sign in sorted({shift % NG, -shift % NG}):
                    picks.append((half, lax.rem(here[half] + sign, NG)))
        lhs = [jnp.concatenate([fa[h, g, j] for h, g in picks], axis=0) for j in range(NX)]
        for which in range(2):
            total = jnp.dot(lhs[0], un[which, 0:DC], preferred_element_type=F32)
            for j in range(1, NX):
                total = total + jnp.dot(lhs[j], un[which, j * DC:(j + 1) * DC], preferred_element_type=F32)
            for n, (h, g) in enumerate(picks):
                lg[which, h, g] = total[n * GR:(n + 1) * GR]

    gain_in[1].wait()
    gain_in[2].wait()
    for half in range(2):
        whole = rcopy(hrow.at[half], hrow.at[half], q_ssem.at[half, 0], q_rsem.at[half], xpeer(1))

        @pl.when(x != lax.rem(here[half], NX))
        def _(whole=whole):
            whole.wait_recv()

        @pl.when(x == lax.rem(here[half], NX))
        def _(half=half):
            for k in far_x:
                rcopy(hrow.at[half], hrow.at[half], q_ssem.at[half, k - 1], q_rsem.at[half], xpeer(k)).wait_send()

    for half in range(2):
        for k in near_x:
            bx_cp[half, k].wait_recv()
        branches = [bx[half, j].astype(F32) for j in range(NX)]
        square = sum(jnp.sum(b * b, axis=1, keepdims=True) for b in branches)
        factor = lax.rsqrt(square / D + EPS)
        square = jnp.zeros((GR, 1), F32)
        for j in range(NX):
            stream = hrow[half, j].astype(F32) + branches[j] * factor * gain(1, j)
            flow[half, j] = stream
            square = square + jnp.sum(stream * stream, axis=1, keepdims=True)
        inverse = lax.rsqrt(square / D + EPS)
        for j in range(NX):
            fa[half, here[half], j] = (flow[half, j] * inverse * gain(2, j)).astype(BF)
            ring(0, j, (half,))

    for s in range(NG // 2):
        for i in range(pieces if s else 0):
            ring(s, i)
        if s == 0:
            w_in[3].wait()
            w_out[3].wait_recv()
    for k in range(1, NX):
        t_cp[k].wait_recv()
    tok_cols = [jnp.sum(jnp.where(eye_low, tk[j, 0:1], 0.0), axis=1, keepdims=True) for j in range(NX)]
    multiply([0, 1] if last > 0 else [0])
    drain(keep=40)
    for s in range(2, NG // 2):
        multiply([s])
    multiply([NG // 2])
    HR = LIVE // 2
    entry = lax.broadcasted_iota(jnp.int32, (NG * GR, VS), 1).astype(F32)
    totals = []
    targets = []
    for half in range(2):
        tok_half = jnp.concatenate(
            [t[half * HR + e * GR:half * HR + (e + 1) * GR] for e in range(E) for t in tok_cols], axis=0
        )
        total = jnp.zeros((NG * GR, 1), F32)
        target = jnp.zeros((NG * GR, 1), F32)
        for which in range(2):
            logits = lg[which, half].reshape(NG * GR, VS)
            capped = CAP * jnp.tanh(logits / CAP)
            offset = (((x * 2 + which) * NZ + z) * NY + y) * VS
            total = total + jnp.sum(jnp.exp(capped - CAP), axis=1, keepdims=True)
            target = target + jnp.sum(
                jnp.where(entry == tok_half - offset.astype(F32), capped, 0.0), axis=1, keepdims=True
            )
        totals.append(total)
        targets.append(target)

    for j in range(NX):
        spans = [(half, (e * NX + j) * GR) for half in range(2) for e in range(E)]
        t = jnp.concatenate([totals[half][at:at + GR] for half, at in spans], axis=0)
        g = jnp.concatenate([targets[half][at:at + GR] for half, at in spans], axis=0)
        row = jnp.sum(jnp.where(eye_low, t, 0.0) + jnp.where(eye_high, g, 0.0), axis=0, keepdims=True)
        fs[j] = jnp.broadcast_to(row, (8, TOK))
    fx_cp = {}
    for k in far_x:
        fx_cp[k] = go(rcopy(fs.at[lax.rem(x + k, NX)], fx.at[k - 1], fx_ssem.at[k - 1], fx_rsem.at[k - 1], xpeer(k)))
    acc = fs[x]
    for k in near_x:
        fx_cp[k].wait_recv()
        acc = acc + fx[k - 1]
    drain(keep=3)
    fyb[...] = acc
    fy_cp = {}
    for k in far_y:
        fy_cp[k] = go(rcopy(fyb, fy.at[k - 1], fy_ssem.at[k - 1], fy_rsem.at[k - 1], ypeer(k)))
    for k in near_first(NY):
        fy_cp[k].wait_recv()
        acc = acc + fy[k - 1]
    fzb[...] = acc
    fz_cp = {}
    for k in far_y:
        fz_cp[k] = go(rcopy(fzb, fz.at[k - 1], fz_ssem.at[k - 1], fz_rsem.at[k - 1], zpeer(k)))
    for k in near_first(NY):
        fz_cp[k].wait_recv()
        acc = acc + fz[k - 1]
    row = acc[0:1]
    t = jnp.sum(jnp.where(eye_low, row, 0.0), axis=1, keepdims=True)
    g = jnp.sum(jnp.where(eye_high, row, 0.0), axis=1, keepdims=True)
    logprob = g - CAP - jnp.log(t)
    out_ref[...] = jnp.sum(jnp.where(pick, logprob, 0.0), axis=0, keepdims=True)
    drain()


def solution(mesh):
    NX = mesh.shape["dp"] // 2
    NY = mesh.shape["vocab"]
    NZ = mesh.shape["tensor"]

    def on_device(
        hidden_in, norm_pre, w_gate, w_up, w_down, norm_post, norm_final, unembed, token_ids, lengths
    ):
        TOK, D = hidden_in.shape
        U = w_gate.shape[1]
        VS = unembed.shape[1]
        DC = D // NX
        DH = DC // 2
        NG = NY
        GR = NX * LIVE // (2 * NG)
        E = NG // NX
        cfg = (NX, NY, NZ, D, U, VS)
        any_spec = pl.BlockSpec(memory_space=pl.ANY)
        vmem = pl.BlockSpec(memory_space=pltpu.VMEM)
        dma = lambda *s: pltpu.SemaphoreType.DMA(s)
        xs = NX - 1
        ys = NY - 1
        pairs = lambda *s: [dma(*s), dma(*s)]
        lines = lambda v: v.reshape(D // 128, 128)
        out = pl.pallas_call(
            functools.partial(kernel, cfg),
            out_shape=jax.ShapeDtypeStruct((1, TOK), F32),
            in_specs=[any_spec] * 10,
            out_specs=vmem,
            scratch_shapes=[
                pltpu.VMEM((TOK, D), BF),
                pltpu.VMEM((3, D // 128, 128), F32),
                pltpu.VMEM((1, TOK), jnp.int32),
                pltpu.SMEM((2,), jnp.int32),
                pltpu.VMEM((xs, 2 * E, GR, DC), BF),
                pltpu.VMEM((NX, 2 * E, GR, DC), BF),
                pltpu.VMEM((2, 2 * U, DH), BF),
                pltpu.VMEM((2, U, DH), BF),
                pltpu.VMEM((U, DC), BF),
                pltpu.VMEM((2, D, VS), BF),
                pltpu.VMEM((LIVE, 2 * U), F32),
                pltpu.VMEM((xs, LIVE, 2 * U), BF),
                pltpu.VMEM((xs, LIVE, 2 * U), BF),
                pltpu.VMEM((NX, LIVE, U), BF),
                pltpu.VMEM((2, NG, GR, DC), BF),
                pltpu.VMEM((2, ys, GR, DC), BF),
                pltpu.VMEM((2, GR, DC), BF),
                pltpu.VMEM((2, ys, GR, DC), BF),
                pltpu.VMEM((2, NX, GR, DC), BF),
                pltpu.VMEM((2, NX, GR, DC), BF),
                pltpu.VMEM((2, NX, GR, DC), F32),
                pltpu.VMEM((2, NG, NX, GR, DC), BF),
                pltpu.VMEM((2, 2, NG, GR, VS), F32),
                pltpu.VMEM((NX, 8, TOK), F32),
                pltpu.VMEM((NX, 8, TOK), F32),
                pltpu.VMEM((xs, 8, TOK), F32),
                pltpu.VMEM((8, TOK), F32),
                pltpu.VMEM((ys, 8, TOK), F32),
                pltpu.VMEM((8, TOK), F32),
                pltpu.VMEM((ys, 8, TOK), F32),
                dma(NX + 9),
            ]
            + pairs(4) + pairs(xs) + pairs(xs) + pairs(xs) + pairs(xs)
            + pairs(2, ys) + pairs(2, ys) + pairs(2, xs) + [dma(2, xs), dma(2)]
            + pairs(2, NG // 2, NX, 2) + pairs(xs) + pairs(ys) + pairs(ys),
            compiler_params=pltpu.CompilerParams(
                collective_id=0, has_side_effects=True, vmem_limit_bytes=60 * 1024 * 1024
            ),
            name="rollout_logprob",
        )(
            hidden_in, lines(norm_pre), lines(norm_post), lines(norm_final), w_gate.T, w_up.T, w_down, unembed,
            token_ids.reshape(1, TOK), lengths,
        )
        return out.reshape(TOK)

    in_specs = (
        P("dp", None),
        P(),
        P("dp", ("tensor", "vocab")),
        P("dp", ("tensor", "vocab")),
        P(("tensor", "vocab"), "dp"),
        P(),
        P(),
        P(None, ("dp", "tensor", "vocab")),
        P("dp"),
        P("dp"),
    )
    return jax.shard_map(
        on_device, mesh=mesh, in_specs=in_specs, out_specs=P("dp"), check_vma=False
    )
```
